32 devices in a mesh: groups: 2 (over y), dp: 4 (over x, core), mp: 4 (over z).
Axes of the slice: x: 2, y: 2, z: 4, core: 2. Of those that a mesh axis runs over, the one named last changes fastest.
Arguments:
- attn_out: bfloat16 [4096, 8192], P(('groups', 'dp'), 'mp'), parts along dimension 0, may hold values from -6 to 6
- out_weight: bfloat16 [8192, 8192], P(None, 'mp'), may hold values from -0.0625 to 0.0625
- cotangent: bfloat16 [4096, 8192], P(('groups', 'dp'), 'mp'), parts along dimension 0, may hold values from -6 to 6
- proj_in_w: bfloat16 [8192, 64], replicated, may hold values from -0.0625 to 0.0625
- proj_out_w: bfloat16 [8192, 64], replicated, may hold values from -0.0625 to 0.0625
- queries: bfloat16 [1024, 4096], P('mp', 'dp'), may hold values from -0.005859375 to 0.005859375
- lengths: int32 [16], P(('groups', 'dp')), parts along dimension 0, may hold values from 1 to 256, 1536 in all
Outputs:
- layer_out: bfloat16 [4096, 8192], P(('groups', 'dp'), 'mp'), parts along dimension 0
- grad_in: bfloat16 [4096, 8192], P(('groups', 'dp'), 'mp'), parts along dimension 0
- scores: float32 [16, 1024], P(('groups', 'dp'), 'mp'), parts along dimension 0
The draws below stay inside these ranges and needn't reach their ends.
There are 2 independent parts, one for each index of `groups`. The reference program is written for one: setup_inputs(seed, part) draws one part's arguments, and reference() takes and returns one part's arrays. A program takes and returns all parts, laid end to end along the dimension named above; an argument that names none is the same for every part. Nothing has to cross between parts.
Inputs may be any that keep to these rules, and one draw needn't show every extreme that they name: Live tokens sit at the start of a sequence; some sequence of each part has exactly 256; the lengths of one part sum to 1536.
All inputs are finite; a program needn't handle non-finite values. No bound on the sum of `lengths` on one device may be relied on, other than what follows from the above.
Results may differ from the reference program's by a relative error of at most 0.001.
Values may be sent and summed in bfloat16 or wider, within the bound.
A program may use at most 192 MiB of HBM per device.

```python
import math
import jax
import jax.numpy as jnp
import numpy as np
from jax import lax

D = 8192
R = 64
NQ = 1024
LEN = 256
EXAMPLES = 8
TOKENS = 2048


def steps_of(stream_key, extent, shards, low, largest):
    def one(dim, blocks):
        steps = jax.random.uniform(jax.random.fold_in(jax.random.fold_in(stream_key, 6), dim), (blocks,), jnp.float32, low / len(shards), largest / len(shards))
        return jnp.repeat(jnp.exp(steps), extent[dim] // blocks).reshape((-1,) + (1,) * (len(extent) - dim - 1))

    gain = one(*shards[0])
    for cut in shards[1:]:
        gain = gain * one(*cut)
    return gain


def length_profile(count, total, reach, slope):
    weights = [(1 << 20) // math.isqrt(standing ** slope) + 1 for standing in range(2, count + 1)]
    spare, given = total - reach - (count - 1), [1] * (count - 1)
    while spare > 0:
        free = [i for i in range(count - 1) if given[i] < reach]
        pool, budget = sum([weights[i] for i in free]), spare
        for i in free:
            extra = min(reach - given[i], max(1, budget * weights[i] // pool), spare)
            given[i] = given[i] + extra
            spare = spare - extra
    return np.array([reach] + given)


def ragged(stream_key, number_of, total, bound, slope):
    if number_of == 2:
        one = jax.random.randint(stream_key, (), max(1, total - bound), min(bound, total - 1) + 1)
        return jnp.stack([one, total - one])
    sizes = jnp.asarray(length_profile(number_of, total, bound, slope), jnp.int32)
    pairs = (number_of - 1) // 2
    giver, sink = sizes[1:1 + 2 * pairs:2], sizes[2:2 + 2 * pairs:2]
    margin = jnp.minimum(giver - 1, bound - sink)
    passed = jax.random.randint(jax.random.fold_in(stream_key, 1), (pairs,), 0, 1 << 20) % (margin + 1)
    sizes = sizes.at[1:1 + 2 * pairs:2].set(giver - passed).at[2:2 + 2 * pairs:2].set(sink + passed)
    return sizes[jax.random.permutation(jax.random.fold_in(stream_key, 2), number_of)]


def centred(rng, shape, scale, most, shards=(), held_as=jnp.bfloat16):
    loudness = steps_of(rng, shape, shards, -0.22, 0.18) if shards else 1.0
    array = jax.random.normal(rng, shape, jnp.float32) * scale * loudness
    return jnp.minimum(jnp.maximum(array, -most), most).astype(held_as)


def setup_inputs(seed: int = 0, part: int = 0) -> dict:
    splits = jax.random.split(jax.random.key(seed), 8)
    part_keys = jax.random.split(jax.random.fold_in(splits[7], part), 8)
    attn_out = centred(part_keys[0], (TOKENS, D), 1.0, 6.0, ((0, 4), (1, 4)))
    out_weight = centred(splits[1], (D, D), D ** -0.5, 0.0625, ((1, 4),))
    cotangent = centred(part_keys[2], (TOKENS, D), 1.0, 6.0, ((0, 4), (1, 4)))
    proj_in_w = centred(splits[3], (D, R), D ** -0.5, 0.0625)
    proj_out_w = centred(splits[4], (D, R), D ** -0.5, 0.0625)
    queries = centred(splits[5], (NQ, R * R), (R * R * LEN) ** -0.5, 0.005859375, ((0, 4), (1, 4)))
    lengths = ragged(part_keys[6], EXAMPLES, EXAMPLES * LEN * 3 // 4, LEN, 1).astype(jnp.int32)
    return dict(attn_out=attn_out, out_weight=out_weight, cotangent=cotangent, proj_in_w=proj_in_w, proj_out_w=proj_out_w, queries=queries, lengths=lengths)


def reference(attn_out, out_weight, cotangent, proj_in_w, proj_out_w, queries, lengths):
    layer_out = jnp.dot(attn_out, out_weight, preferred_element_type=jnp.float32).astype(jnp.bfloat16)
    grad_in = lax.dot_general(cotangent, out_weight, (((1,), (1,)), ((), ())),
                              preferred_element_type=jnp.float32).astype(jnp.bfloat16)
    proj_in = jnp.dot(attn_out, proj_in_w, preferred_element_type=jnp.float32)
    proj_out = jnp.dot(cotangent, proj_out_w, preferred_element_type=jnp.float32)
    slot_index = jnp.arange(TOKENS, dtype=jnp.int32)
    example_ids = slot_index // LEN
    positions = slot_index % LEN
    live = (positions < lengths[example_ids]).astype(jnp.float32)
    weighted = (proj_in * live[:, None]).reshape(EXAMPLES, LEN, R)
    kronecker = jnp.einsum("eti,etj->eij", weighted, proj_out.reshape(EXAMPLES, LEN, R),
                           precision=lax.Precision.HIGHEST).reshape(EXAMPLES, R * R)
    scores = jnp.dot(kronecker, queries.astype(jnp.float32).T, precision=lax.Precision.HIGHEST)
    return layer_out, grad_in, scores
```

```python
import functools

import jax
import jax.numpy as jnp
from jax import lax
from jax.experimental import pallas as pl
from jax.experimental.pallas import tpu as pltpu
from jax.sharding import PartitionSpec as P

LEN = 256
CHUNKS = 2
STEPS = 32767.0
MESH = pl.DeviceIdType.MESH

HIGHEST_PRECISION = lax.Precision.HIGHEST


def kernel(n, narrow, attn_hbm, cot_hbm, w_hbm, lay_ref, grad_ref, gath, cot, wbuf, acc, gacc, tmp, rs, stage,
           sc, sstage, in_sem, w_sem, ag_recv, ag_send_r, ag_send_l, rs_recv, rs_send, sc_recv, sc_send):
    me = lax.axis_index("mp")
    tok, bw = cot.shape
    cr = tok // CHUNKS
    tn = min(256, bw)
    tiles = bw // tn

    def rows_of(c):
        return pl.ds(pl.multiple_of(c * cr, cr), cr)

    def cols_of(t):
        return pl.ds(pl.multiple_of(t * tn, tn), tn)

    def w_load(block, slot):
        return pltpu.make_async_copy(
            w_hbm.at[pl.ds(pl.multiple_of(block * bw, bw), bw), :], wbuf.at[slot], w_sem.at[slot])

    attn_in = pltpu.make_async_copy(attn_hbm, gath.at[me], in_sem.at[0])
    cot_in = pltpu.make_async_copy(cot_hbm, cot, in_sem.at[1])
    attn_in.start()
    cot_in.start()

    barrier = pltpu.get_barrier_semaphore()
    has_left, has_right = me > 0, me < n - 1

    @pl.when(has_left)
    def _():
        pl.semaphore_signal(barrier, inc=1, device_id={"mp": me - 1}, device_id_type=MESH)

    @pl.when(has_right)
    def _():
        pl.semaphore_signal(barrier, inc=1, device_id={"mp": me + 1}, device_id_type=MESH)

    pl.semaphore_wait(barrier, has_left.astype(jnp.int32) + has_right.astype(jnp.int32))

    def ag_copy(origin, c, side):
        part = gath.at[origin, rows_of(c)]
        sems = ag_send_r if side > 0 else ag_send_l
        return pltpu.make_async_remote_copy(
            src_ref=part, dst_ref=part, send_sem=sems.at[origin, c], recv_sem=ag_recv.at[origin, c],
            device_id={"mp": me + side}, device_id_type=MESH)

    def ag_wait(origin, c):
        part = gath.at[origin, rows_of(c)]
        pltpu.make_async_copy(part, part, ag_recv.at[origin, c]).wait()

    def rs_copies(d, c, side):
        out = d - 1 if side > 0 else d
        there = d if side > 0 else jnp.where(d == me - 1, n, d)
        data = pltpu.make_async_remote_copy(
            src_ref=stage.at[out, rows_of(c)], dst_ref=rs.at[there, rows_of(c)],
            send_sem=rs_send.at[out, c], recv_sem=rs_recv.at[there, c],
            device_id={"mp": me + side}, device_id_type=MESH)
        if not narrow:
            return (data,)
        return (data, pltpu.make_async_remote_copy(
            src_ref=sstage.at[out, c], dst_ref=sc.at[there, c],
            send_sem=sc_send.at[out, c], recv_sem=sc_recv.at[there, c],
            device_id={"mp": me + side}, device_id_type=MESH))

    def rs_wait(slot, c):
        pltpu.make_async_copy(rs.at[slot, rows_of(c)], rs.at[slot, rows_of(c)], rs_recv.at[slot, c]).wait()
        if narrow:
            pltpu.make_async_copy(sc.at[slot, c], sc.at[slot, c], sc_recv.at[slot, c]).wait()

    def scale_of(slot, c):
        wide = jnp.broadcast_to(sc[slot, c][0:1, :], (128, cr))
        return jnp.transpose(wide)[:, 0:1] * (1.0 / STEPS)

    attn_in.wait()
    for c in range(CHUNKS):
        @pl.when(has_right)
        def _():
            ag_copy(me, c, 1).start()

        @pl.when(has_left)
        def _():
            ag_copy(me, c, -1).start()
    cot_in.wait()

    def partial_tile(slot, rows, t):
        return lax.dot_general(
            cot[rows, :], wbuf[slot, cols_of(t), :], (((1,), (1,)), ((), ())),
            preferred_element_type=jnp.float32)

    def rs_task(d, c, side, slot, incoming):
        rows = rows_of(c)
        src = d

        def first(t, top):
            tmp[:, cols_of(t)] = partial_tile(slot, rows, t)
            return top

        lax.fori_loop(0, tiles, first, 0)

        @pl.when(incoming)
        def _():
            rs_wait(src, c)
            scale = scale_of(src, c) if narrow else 1.0

            def add(t, top):
                tmp[:, cols_of(t)] += rs[src, rows, cols_of(t)].astype(jnp.float32) * scale
                return top

            lax.fori_loop(0, tiles, add, 0)

        out = d - 1 if side > 0 else d
        if narrow:
            def most(t, top):
                part = jnp.abs(tmp[:, cols_of(t)])
                for k in range(tn // 128):
                    top = jnp.maximum(top, part[:, k * 128:(k + 1) * 128])
                return top

            top = lax.fori_loop(0, tiles, most, jnp.full((cr, 128), 1e-30, jnp.float32))
            sstage[out, c] = jnp.broadcast_to(jnp.max(jnp.transpose(top), axis=0, keepdims=True), (8, cr))
            inv = STEPS / jnp.max(top, axis=1, keepdims=True)

            def code(t, top):
                stage[out, rows, cols_of(t)] = jnp.round(tmp[:, cols_of(t)] * inv).astype(jnp.int32).astype(jnp.int16)
                return top
        else:
            def code(t, top):
                stage[out, rows, cols_of(t)] = tmp[:, cols_of(t)]
                return top

        lax.fori_loop(0, tiles, code, 0)
        for copy in rs_copies(d, c, side):
            copy.start()

    def rs_last(c, slot):
        rows = rows_of(c)
        rs_wait(slot, c)
        scale = scale_of(slot, c) if narrow else 1.0

        def add(t, top):
            gacc[rows, cols_of(t)] += rs[slot, rows, cols_of(t)].astype(jnp.float32) * scale
            return top

        lax.fori_loop(0, tiles, add, 0)

    def forward(origin, slot, fresh=False):
        def body(t, top):
            part = jnp.dot(gath[origin], wbuf[slot, :, cols_of(t)], preferred_element_type=jnp.float32)
            if fresh:
                acc[:, cols_of(t)] = part
            else:
                acc[:, cols_of(t)] += part
            return top

        lax.fori_loop(0, tiles, body, 0)

    def own():
        load = w_load(me, 0)
        load.start()
        load.wait()

        def body(t, top):
            gacc[:, cols_of(t)] = partial_tile(0, slice(None), t)
            return top

        lax.fori_loop(0, tiles, body, 0)
        forward(me, 0, True)

    def ring(r, top):
        from_left, from_right = me - r, me + r
        ag_l, ag_r = (r > 0) & (from_left >= 0), (r > 0) & (from_right < n)
        d_r = jnp.where(has_left, n - r, n - 1 - r)
        d_l = jnp.where(has_right, r - 1, r)
        turn = (r > 0)
        send_r = has_right & (d_r > me) & (turn | (me == 0))
        send_l = has_left & (d_l < me) & (turn | (me == n - 1))
        last_r = has_left & turn & (d_r == me)
        last_l = has_right & turn & (d_l == me)

        @pl.when(send_r)
        def _():
            w_load(d_r, 0).start()

        @pl.when(send_l)
        def _():
            w_load(d_l, 1).start()

        @pl.when(send_r)
        def _():
            w_load(d_r, 0).wait()

        @pl.when(send_l)
        def _():
            w_load(d_l, 1).wait()

        def chunk(c, top):
            @pl.when(ag_l)
            def _():
                ag_wait(from_left, c)

                @pl.when(has_right)
                def _():
                    ag_copy(from_left, c, 1).start()

            @pl.when(ag_r)
            def _():
                ag_wait(from_right, c)

                @pl.when(has_left)
                def _():
                    ag_copy(from_right, c, -1).start()

            @pl.when(send_r)
            def _():
                rs_task(d_r, c, 1, 0, has_left)

            @pl.when(send_l)
            def _():
                rs_task(d_l, c, -1, 1, has_right)

            return top

        lax.fori_loop(0, CHUNKS, chunk, 0)

        @pl.when(ag_l)
        def _():
            w_load(from_left, 0).start()

        @pl.when(ag_r)
        def _():
            w_load(from_right, 1).start()

        @pl.when(r == 0)
        def _():
            own()

        @pl.when(ag_l)
        def _():
            w_load(from_left, 0).wait()
            forward(from_left, 0)

        @pl.when(ag_r)
        def _():
            w_load(from_right, 1).wait()
            forward(from_right, 1)

        def finish(c, top):
            @pl.when(last_r)
            def _():
                rs_last(c, me)

            @pl.when(last_l)
            def _():
                rs_last(c, n)

            return top

        lax.fori_loop(0, CHUNKS, finish, 0)
        return top

    lax.fori_loop(0, n, ring, 0)

    def result(t, top):
        lay_ref[:, cols_of(t)] = acc[:, cols_of(t)].astype(lay_ref.dtype)
        grad_ref[:, cols_of(t)] = gacc[:, cols_of(t)].astype(grad_ref.dtype)
        return top

    lax.fori_loop(0, tiles, result, 0)

    def drain(o, top):
        for c in range(CHUNKS):
            @pl.when(has_right & (o <= me))
            def _():
                ag_copy(o, c, 1).wait_send()

            @pl.when(has_left & (o >= me))
            def _():
                ag_copy(o, c, -1).wait_send()

            @pl.when(o > me)
            def _():
                for copy in rs_copies(o, c, 1):
                    copy.wait_send()

            @pl.when(o < me)
            def _():
                for copy in rs_copies(o, c, -1):
                    copy.wait_send()
        return top

    lax.fori_loop(0, n, drain, 0)


def both_products(n, attn_out, cotangent, out_weight):
    tok, bw = attn_out.shape
    narrow = n <= 8
    wire = jnp.int16 if narrow else jnp.float32
    cr = tok // CHUNKS
    dma = pltpu.SemaphoreType.DMA
    out = jax.ShapeDtypeStruct((tok, bw), jnp.bfloat16)
    return pl.pallas_call(
        functools.partial(kernel, n, narrow),
        out_shape=(out, out),
        in_specs=[pl.BlockSpec(memory_space=pl.ANY)] * 3,
        out_specs=(pl.BlockSpec(memory_space=pltpu.VMEM),) * 2,
        scratch_shapes=[
            pltpu.VMEM((n, tok, bw), jnp.bfloat16),
            pltpu.VMEM((tok, bw), jnp.bfloat16),
            pltpu.VMEM((2, bw, bw), jnp.bfloat16),
            pltpu.VMEM((tok, bw), jnp.float32),
            pltpu.VMEM((tok, bw), jnp.float32),
            pltpu.VMEM((cr, bw), jnp.float32),
            pltpu.VMEM((n + 1, tok, bw), wire),
            pltpu.VMEM((n - 1, tok, bw), wire),
            pltpu.VMEM((n + 1, CHUNKS, 8, cr), jnp.float32),
            pltpu.VMEM((n - 1, CHUNKS, 8, cr), jnp.float32),
            dma((2,)),
            dma((2,)),
            dma((n, CHUNKS)),
            dma((n, CHUNKS)),
            dma((n, CHUNKS)),
            dma((n + 1, CHUNKS)),
            dma((n - 1, CHUNKS)),
            dma((n + 1, CHUNKS)),
            dma((n - 1, CHUNKS)),
        ],
        compiler_params=pltpu.CompilerParams(
            collective_id=0, has_side_effects=True, vmem_limit_bytes=62 * 1024 * 1024
        ),
        cost_estimate=pl.CostEstimate(
            flops=4 * n * tok * bw * bw, bytes_accessed=400 * 1024 * 1024, transcendentals=0
        ),
    )(attn_out, cotangent, out_weight)


def per_device(n, attn_out, out_weight, cotangent, proj_in_w, proj_out_w, queries, lengths):
    tok_rows = attn_out.shape[0]
    block_width = attn_out.shape[1]
    rank_width = proj_in_w.shape[1]
    seq_count = lengths.shape[0]
    block_start = lax.axis_index("mp") * block_width
    local_in_w = lax.dynamic_slice_in_dim(proj_in_w, block_start, block_width, 0)
    local_out_w = lax.dynamic_slice_in_dim(proj_out_w, block_start, block_width, 0)
    part_in = jnp.dot(attn_out, local_in_w, preferred_element_type=jnp.float32)
    part_out = jnp.dot(cotangent, local_out_w, preferred_element_type=jnp.float32)
    proj_in, proj_out = lax.psum((part_in, part_out), "mp")
    layer_out, grad_in = both_products(n, attn_out, cotangent, out_weight)
    slot_index = jnp.arange(tok_rows, dtype=jnp.int32)
    example_ids = slot_index // LEN
    offsets = slot_index % LEN
    seq_slots = jnp.arange(seq_count, dtype=jnp.int32)
    live_table = (example_ids[:, None] == seq_slots[None, :]) & (
        offsets[:, None] < lengths[None, :]
    )
    live_rows = jnp.sum(live_table.astype(jnp.float32), axis=1)
    weighted = (proj_in * live_rows[:, None]).reshape(seq_count, LEN, rank_width)
    kronecker = jnp.einsum(
        "eti,etj->eij",
        weighted,
        proj_out.reshape(seq_count, LEN, rank_width),
        precision=HIGHEST_PRECISION,
    ).reshape(seq_count, rank_width * rank_width)
    scores = lax.dot_general(
        kronecker,
        lax.all_gather(queries, "dp", axis=1, tiled=True).astype(jnp.float32),
        (((1,), (1,)), ((), ())),
        precision=HIGHEST_PRECISION,
        preferred_element_type=jnp.float32,
    )
    return (layer_out, grad_in, scores)


def solution(mesh):
    in_specs = (
        P(("groups", "dp"), "mp"),
        P(None, "mp"),
        P(("groups", "dp"), "mp"),
        P(),
        P(),
        P("mp", "dp"),
        P(("groups", "dp")),
    )
    out_specs = (P(("groups", "dp"), "mp"), P(("groups", "dp"), "mp"), P(("groups", "dp"), "mp"))
    return jax.shard_map(
        functools.partial(per_device, mesh.shape["mp"]),
        mesh=mesh, in_specs=in_specs, out_specs=out_specs, check_vma=False,
    )
```

```python
import functools

import jax
import jax.numpy as jnp
from jax import lax
from jax.experimental import pallas as pl
from jax.experimental.pallas import tpu as pltpu
from jax.sharding import PartitionSpec as P

LEN = 256
CHUNKS = 4
STEPS = 32767.0
MESH = pl.DeviceIdType.MESH

HIGHEST_PRECISION = lax.Precision.HIGHEST


def kernel(n, narrow, attn_hbm, cot_hbm, w_hbm, lay_ref, grad_ref, gath, cot, wbuf, acc, gacc, tmp, rs, stage,
           sc, sstage, in_sem, w_sem, ag_recv, ag_send_r, ag_send_l, rs_recv, rs_send, sc_recv, sc_send):
    me = lax.axis_index("mp")
    tok, bw = cot.shape
    cr = tok // CHUNKS
    tn = min(256, bw)
    tiles = bw // tn

    def rows_of(c):
        return pl.ds(pl.multiple_of(c * cr, cr), cr)

    def cols_of(t):
        return pl.ds(pl.multiple_of(t * tn, tn), tn)

    def w_load(block, slot):
        return pltpu.make_async_copy(
            w_hbm.at[pl.ds(pl.multiple_of(block * bw, bw), bw), :], wbuf.at[slot], w_sem.at[slot])

    attn_in = pltpu.make_async_copy(attn_hbm, gath.at[me], in_sem.at[0])
    cot_in = pltpu.make_async_copy(cot_hbm, cot, in_sem.at[1])
    attn_in.start()
    cot_in.start()

    barrier = pltpu.get_barrier_semaphore()
    has_left, has_right = me > 0, me < n - 1

    @pl.when(has_left)
    def _():
        pl.semaphore_signal(barrier, inc=1, device_id={"mp": me - 1}, device_id_type=MESH)

    @pl.when(has_right)
    def _():
        pl.semaphore_signal(barrier, inc=1, device_id={"mp": me + 1}, device_id_type=MESH)

    pl.semaphore_wait(barrier, has_left.astype(jnp.int32) + has_right.astype(jnp.int32))

    def ag_copy(origin, c, side):
        part = gath.at[origin, rows_of(c)]
        sems = ag_send_r if side > 0 else ag_send_l
        return pltpu.make_async_remote_copy(
            src_ref=part, dst_ref=part, send_sem=sems.at[origin, c], recv_sem=ag_recv.at[origin, c],
            device_id={"mp": me + side}, device_id_type=MESH)

    def ag_wait(origin, c):
        part = gath.at[origin, rows_of(c)]
        pltpu.make_async_copy(part, part, ag_recv.at[origin, c]).wait()

    def rs_copies(d, c, side):
        out = d - 1 if side > 0 else d
        there = d if side > 0 else jnp.where(d == me - 1, n, d)
        data = pltpu.make_async_remote_copy(
            src_ref=stage.at[out, rows_of(c)], dst_ref=rs.at[there, rows_of(c)],
            send_sem=rs_send.at[out, c], recv_sem=rs_recv.at[there, c],
            device_id={"mp": me + side}, device_id_type=MESH)
        if not narrow:
            return (data,)
        return (data, pltpu.make_async_remote_copy(
            src_ref=sstage.at[out, c], dst_ref=sc.at[there, c],
            send_sem=sc_send.at[out, c], recv_sem=sc_recv.at[there, c],
            device_id={"mp": me + side}, device_id_type=MESH))

    def rs_wait(slot, c):
        pltpu.make_async_copy(rs.at[slot, rows_of(c)], rs.at[slot, rows_of(c)], rs_recv.at[slot, c]).wait()
        if narrow:
            pltpu.make_async_copy(sc.at[slot, c], sc.at[slot, c], sc_recv.at[slot, c]).wait()

    def scale_of(slot, c):
        wide = jnp.broadcast_to(sc[slot, c][0:1, :], (128, cr))
        return jnp.transpose(wide)[:, 0:1] * (1.0 / STEPS)

    attn_in.wait()
    for c in range(CHUNKS):
        @pl.when(has_right)
        def _():
            ag_copy(me, c, 1).start()

        @pl.when(has_left)
        def _():
            ag_copy(me, c, -1).start()
    cot_in.wait()

    def partial_tile(slot, rows, t):
        return lax.dot_general(
            cot[rows, :], wbuf[slot, cols_of(t), :], (((1,), (1,)), ((), ())),
            preferred_element_type=jnp.float32)

    def rs_task(d, c, side, slot, incoming, opening):
        rows = rows_of(c)
        src = d

        def first(t, top):
            tmp[:, cols_of(t)] = partial_tile(slot, rows, t)
            return top

        lax.fori_loop(0, tiles, first, 0)

        @pl.when(incoming)
        def _():
            rs_wait(src, c)
            scale = scale_of(src, c) if narrow else 1.0

            def add(t, top):
                tmp[:, cols_of(t)] += rs[src, rows, cols_of(t)].astype(jnp.float32) * scale
                return top

            lax.fori_loop(0, tiles, add, 0)

        out = d - 1 if side > 0 else d
        if narrow:
            def most(t, top):
                part = jnp.abs(tmp[:, cols_of(t)])
                for k in range(tn // 128):
                    top = jnp.maximum(top, part[:, k * 128:(k + 1) * 128])
                return top

            top = lax.fori_loop(0, tiles, most, jnp.full((cr, 128), 1e-30, jnp.float32))
            sstage[out, c] = jnp.broadcast_to(jnp.max(jnp.transpose(top), axis=0, keepdims=True), (8, cr))
            inv = STEPS / jnp.max(top, axis=1, keepdims=True)

            def code(t, top):
                stage[out, rows, cols_of(t)] = jnp.round(tmp[:, cols_of(t)] * inv).astype(jnp.int32).astype(jnp.int16)
                return top
        else:
            def code(t, top):
                stage[out, rows, cols_of(t)] = tmp[:, cols_of(t)]
                return top

        lax.fori_loop(0, tiles, code, 0)

        @pl.when(opening)
        def _():
            ag_copy(0 if side > 0 else n - 1, c, side).wait_send()

        @pl.when(jnp.logical_not(opening))
        def _():
            for copy in rs_copies(d + side, c, side):
                copy.wait_send()

        for copy in rs_copies(d, c, side):
            copy.start()

    def rs_last(c, slot):
        rows = rows_of(c)
        rs_wait(slot, c)
        scale = scale_of(slot, c) if narrow else 1.0

        def add(t, top):
            gacc[rows, cols_of(t)] += rs[slot, rows, cols_of(t)].astype(jnp.float32) * scale
            return top

        lax.fori_loop(0, tiles, add, 0)

    def forward(origin, slot, fresh=False):
        def body(t, top):
            part = jnp.dot(gath[origin], wbuf[slot, :, cols_of(t)], preferred_element_type=jnp.float32)
            if fresh:
                acc[:, cols_of(t)] = part
            else:
                acc[:, cols_of(t)] += part
            return top

        lax.fori_loop(0, tiles, body, 0)

    def own():
        load = w_load(me, 0)
        load.start()
        load.wait()

        def body(t, top):
            gacc[:, cols_of(t)] = partial_tile(0, slice(None), t)
            return top

        lax.fori_loop(0, tiles, body, 0)
        forward(me, 0, True)

    def ring(r, top):
        from_left, from_right = me - r, me + r
        ag_l, ag_r = (r > 0) & (from_left >= 0), (r > 0) & (from_right < n)
        late_r, late_l = r - me, r - (n - 1 - me)
        d_r, d_l = n - 1 - late_r, late_l
        send_r = (late_r >= 0) & (d_r > me)
        send_l = (late_l >= 0) & (d_l < me)
        last = r == n - 1

        @pl.when(send_r)
        def _():
            w_load(d_r, 0).start()

        @pl.when(send_l)
        def _():
            w_load(d_l, 1).start()

        def pass_on(c, top):
            @pl.when(ag_l)
            def _():
                ag_wait(from_left, c)

                @pl.when(has_right)
                def _():
                    ag_copy(from_left + 1, c, 1).wait_send()
                    ag_copy(from_left, c, 1).start()

            @pl.when(ag_r)
            def _():
                ag_wait(from_right, c)

                @pl.when(has_left)
                def _():
                    ag_copy(from_right - 1, c, -1).wait_send()
                    ag_copy(from_right, c, -1).start()

            return top

        lax.fori_loop(0, CHUNKS, pass_on, 0)

        @pl.when(send_r)
        def _():
            w_load(d_r, 0).wait()

        @pl.when(send_l)
        def _():
            w_load(d_l, 1).wait()

        def chunk(c, top):
            @pl.when(send_r)
            def _():
                rs_task(d_r, c, 1, 0, has_left, late_r == 0)

            @pl.when(send_l)
            def _():
                rs_task(d_l, c, -1, 1, has_right, late_l == 0)

            return top

        lax.fori_loop(0, CHUNKS, chunk, 0)

        @pl.when(ag_l)
        def _():
            w_load(from_left, 0).start()

        @pl.when(ag_r)
        def _():
            w_load(from_right, 1).start()

        @pl.when(ag_l)
        def _():
            w_load(from_left, 0).wait()
            forward(from_left, 0)

        @pl.when(ag_r)
        def _():
            w_load(from_right, 1).wait()
            forward(from_right, 1)

        def finish(c, top):
            @pl.when(last & has_left)
            def _():
                rs_last(c, me)

            @pl.when(last & has_right)
            def _():
                rs_last(c, n)

            return top

        lax.fori_loop(0, CHUNKS, finish, 0)
        return top

    own()
    lax.fori_loop(0, n, ring, 0)

    def result(t, top):
        lay_ref[:, cols_of(t)] = acc[:, cols_of(t)].astype(lay_ref.dtype)
        grad_ref[:, cols_of(t)] = gacc[:, cols_of(t)].astype(grad_ref.dtype)
        return top

    lax.fori_loop(0, tiles, result, 0)

    for c in range(CHUNKS):
        @pl.when(has_right)
        def _():
            for copy in rs_copies(me + 1, c, 1):
                copy.wait_send()

        @pl.when(has_left)
        def _():
            for copy in rs_copies(me - 1, c, -1):
                copy.wait_send()


def both_products(n, attn_out, cotangent, out_weight):
    tok, bw = attn_out.shape
    narrow = n <= 8
    wire = jnp.int16 if narrow else jnp.float32
    cr = tok // CHUNKS
    dma = pltpu.SemaphoreType.DMA
    out = jax.ShapeDtypeStruct((tok, bw), jnp.bfloat16)
    return pl.pallas_call(
        functools.partial(kernel, n, narrow),
        out_shape=(out, out),
        in_specs=[pl.BlockSpec(memory_space=pl.ANY)] * 3,
        out_specs=(pl.BlockSpec(memory_space=pltpu.VMEM),) * 2,
        scratch_shapes=[
            pltpu.VMEM((n, tok, bw), jnp.bfloat16),
            pltpu.VMEM((tok, bw), jnp.bfloat16),
            pltpu.VMEM((2, bw, bw), jnp.bfloat16),
            pltpu.VMEM((tok, bw), jnp.float32),
            pltpu.VMEM((tok, bw), jnp.float32),
            pltpu.VMEM((cr, bw), jnp.float32),
            pltpu.VMEM((n + 1, tok, bw), wire),
            pltpu.VMEM((n - 1, tok, bw), wire),
            pltpu.VMEM((n + 1, CHUNKS, 8, cr), jnp.float32),
            pltpu.VMEM((n - 1, CHUNKS, 8, cr), jnp.float32),
            dma((2,)),
            dma((2,)),
            dma((n, CHUNKS)),
            dma((n, CHUNKS)),
            dma((n, CHUNKS)),
            dma((n + 1, CHUNKS)),
            dma((n - 1, CHUNKS)),
            dma((n + 1, CHUNKS)),
            dma((n - 1, CHUNKS)),
        ],
        compiler_params=pltpu.CompilerParams(
            collective_id=0, has_side_effects=True, vmem_limit_bytes=62 * 1024 * 1024
        ),
        cost_estimate=pl.CostEstimate(
            flops=4 * n * tok * bw * bw, bytes_accessed=400 * 1024 * 1024, transcendentals=0
        ),
    )(attn_out, cotangent, out_weight)


def per_device(n, attn_out, out_weight, cotangent, proj_in_w, proj_out_w, queries, lengths):
    tok_rows = attn_out.shape[0]
    block_width = attn_out.shape[1]
    rank_width = proj_in_w.shape[1]
    seq_count = lengths.shape[0]
    block_start = lax.axis_index("mp") * block_width
    local_in_w = lax.dynamic_slice_in_dim(proj_in_w, block_start, block_width, 0)
    local_out_w = lax.dynamic_slice_in_dim(proj_out_w, block_start, block_width, 0)
    part_in = jnp.dot(attn_out, local_in_w, preferred_element_type=jnp.float32)
    part_out = jnp.dot(cotangent, local_out_w, preferred_element_type=jnp.float32)
    proj_in, proj_out = lax.psum((part_in, part_out), "mp")
    layer_out, grad_in = both_products(n, attn_out, cotangent, out_weight)
    slot_index = jnp.arange(tok_rows, dtype=jnp.int32)
    example_ids = slot_index // LEN
    offsets = slot_index % LEN
    seq_slots = jnp.arange(seq_count, dtype=jnp.int32)
    live_table = (example_ids[:, None] == seq_slots[None, :]) & (
        offsets[:, None] < lengths[None, :]
    )
    live_rows = jnp.sum(live_table.astype(jnp.float32), axis=1)
    weighted = (proj_in * live_rows[:, None]).reshape(seq_count, LEN, rank_width)
    kronecker = jnp.einsum(
        "eti,etj->eij",
        weighted,
        proj_out.reshape(seq_count, LEN, rank_width),
        precision=HIGHEST_PRECISION,
    ).reshape(seq_count, rank_width * rank_width)
    scores = lax.dot_general(
        kronecker,
        lax.all_gather(queries, "dp", axis=1, tiled=True).astype(jnp.float32),
        (((1,), (1,)), ((), ())),
        precision=HIGHEST_PRECISION,
        preferred_element_type=jnp.float32,
    )
    return (layer_out, grad_in, scores)


def solution(mesh):
    in_specs = (
        P(("groups", "dp"), "mp"),
        P(None, "mp"),
        P(("groups", "dp"), "mp"),
        P(),
        P(),
        P("mp", "dp"),
        P(("groups", "dp")),
    )
    out_specs = (P(("groups", "dp"), "mp"), P(("groups", "dp"), "mp"), P(("groups", "dp"), "mp"))
    return jax.shard_map(
        functools.partial(per_device, mesh.shape["mp"]),
        mesh=mesh, in_specs=in_specs, out_specs=out_specs, check_vma=False,
    )
```

```python
import functools

import jax
import jax.numpy as jnp
from jax import lax
from jax.experimental import pallas as pl
from jax.experimental.pallas import tpu as pltpu
from jax.sharding import PartitionSpec as P

LEN = 256
CHUNKS = 4
STEPS = 32767.0
MESH = pl.DeviceIdType.MESH

HIGHEST_PRECISION = lax.Precision.HIGHEST


def kernel(n, narrow, attn_hbm, cot_hbm, w_hbm, pw_ref, lay_ref, grad_ref, pin_ref, gath, cot, wbuf, acc, gacc, tmp, rs, stage,
           sc, sstage, in_sem, w_sem, ag_recv, ag_send_r, ag_send_l, rs_recv, rs_send, sc_recv, sc_send):
    me = lax.axis_index("mp")
    tok, bw = cot.shape
    cr = tok // CHUNKS
    tn = min(256, bw)
    tiles = bw // tn

    def rows_of(c):
        return pl.ds(pl.multiple_of(c * cr, cr), cr)

    def cols_of(t):
        return pl.ds(pl.multiple_of(t * tn, tn), tn)

    def w_load(block, slot):
        return pltpu.make_async_copy(
            w_hbm.at[pl.ds(pl.multiple_of(block * bw, bw), bw), :], wbuf.at[slot], w_sem.at[slot])

    attn_in = pltpu.make_async_copy(attn_hbm, gath.at[me], in_sem.at[0])
    cot_in = pltpu.make_async_copy(cot_hbm, cot, in_sem.at[1])
    attn_in.start()
    cot_in.start()

    barrier = pltpu.get_barrier_semaphore()
    has_left, has_right = me > 0, me < n - 1

    @pl.when(has_left)
    def _():
        pl.semaphore_signal(barrier, inc=1, device_id={"mp": me - 1}, device_id_type=MESH)

    @pl.when(has_right)
    def _():
        pl.semaphore_signal(barrier, inc=1, device_id={"mp": me + 1}, device_id_type=MESH)

    pl.semaphore_wait(barrier, has_left.astype(jnp.int32) + has_right.astype(jnp.int32))

    def ag_copy(origin, c, side):
        part = gath.at[origin, rows_of(c)]
        sems = ag_send_r if side > 0 else ag_send_l
        return pltpu.make_async_remote_copy(
            src_ref=part, dst_ref=part, send_sem=sems.at[origin, c], recv_sem=ag_recv.at[origin, c],
            device_id={"mp": me + side}, device_id_type=MESH)

    def ag_wait(origin, c):
        part = gath.at[origin, rows_of(c)]
        pltpu.make_async_copy(part, part, ag_recv.at[origin, c]).wait()

    def rs_copies(d, c, side):
        out = d - 1 if side > 0 else d
        there = d if side > 0 else jnp.where(d == me - 1, n, d)
        data = pltpu.make_async_remote_copy(
            src_ref=stage.at[out, rows_of(c)], dst_ref=rs.at[there, rows_of(c)],
            send_sem=rs_send.at[out, c], recv_sem=rs_recv.at[there, c],
            device_id={"mp": me + side}, device_id_type=MESH)
        if not narrow:
            return (data,)
        return (data, pltpu.make_async_remote_copy(
            src_ref=sstage.at[out, c], dst_ref=sc.at[there, c],
            send_sem=sc_send.at[out, c], recv_sem=sc_recv.at[there, c],
            device_id={"mp": me + side}, device_id_type=MESH))

    def rs_wait(slot, c):
        pltpu.make_async_copy(rs.at[slot, rows_of(c)], rs.at[slot, rows_of(c)], rs_recv.at[slot, c]).wait()
        if narrow:
            pltpu.make_async_copy(sc.at[slot, c], sc.at[slot, c], sc_recv.at[slot, c]).wait()

    def scale_of(slot, c):
        wide = jnp.broadcast_to(sc[slot, c][0:1, :], (128, cr))
        return jnp.transpose(wide)[:, 0:1] * (1.0 / STEPS)

    attn_in.wait()
    for c in range(CHUNKS):
        @pl.when(has_right)
        def _():
            ag_copy(me, c, 1).start()

        @pl.when(has_left)
        def _():
            ag_copy(me, c, -1).start()
    cot_in.wait()

    def partial_tile(slot, rows, t):
        return lax.dot_general(
            cot[rows, :], wbuf[slot, cols_of(t), :], (((1,), (1,)), ((), ())),
            preferred_element_type=jnp.float32)

    def rs_task(d, c, side, slot, incoming, opening):
        rows = rows_of(c)
        src = d

        def first(t, top):
            tmp[:, cols_of(t)] = partial_tile(slot, rows, t)
            return top

        lax.fori_loop(0, tiles, first, 0)

        @pl.when(incoming)
        def _():
            rs_wait(src, c)
            scale = scale_of(src, c) if narrow else 1.0

            def add(t, top):
                tmp[:, cols_of(t)] += rs[src, rows, cols_of(t)].astype(jnp.float32) * scale
                return top

            lax.fori_loop(0, tiles, add, 0)

        out = d - 1 if side > 0 else d
        if narrow:
            def most(t, top):
                part = jnp.abs(tmp[:, cols_of(t)])
                for k in range(tn // 128):
                    top = jnp.maximum(top, part[:, k * 128:(k + 1) * 128])
                return top

            top = lax.fori_loop(0, tiles, most, jnp.full((cr, 128), 1e-30, jnp.float32))
            sstage[out, c] = jnp.broadcast_to(jnp.max(jnp.transpose(top), axis=0, keepdims=True), (8, cr))
            inv = STEPS / jnp.max(top, axis=1, keepdims=True)

            def code(t, top):
                stage[out, rows, cols_of(t)] = jnp.round(tmp[:, cols_of(t)] * inv).astype(jnp.int32).astype(jnp.int16)
                return top
        else:
            def code(t, top):
                stage[out, rows, cols_of(t)] = tmp[:, cols_of(t)]
                return top

        lax.fori_loop(0, tiles, code, 0)

        @pl.when(opening)
        def _():
            ag_copy(0 if side > 0 else n - 1, c, side).wait_send()

        @pl.when(jnp.logical_not(opening))
        def _():
            for copy in rs_copies(d + side, c, side):
                copy.wait_send()

        for copy in rs_copies(d, c, side):
            copy.start()

    def rs_last(c, slot):
        rows = rows_of(c)
        rs_wait(slot, c)
        scale = scale_of(slot, c) if narrow else 1.0

        def add(t, top):
            gacc[rows, cols_of(t)] += rs[slot, rows, cols_of(t)].astype(jnp.float32) * scale
            return top

        lax.fori_loop(0, tiles, add, 0)

    def forward(origin, slot, fresh=False):
        def body(t, top):
            part = jnp.dot(gath[origin], wbuf[slot, :, cols_of(t)], preferred_element_type=jnp.float32)
            if fresh:
                acc[:, cols_of(t)] = part
            else:
                acc[:, cols_of(t)] += part
            return top

        lax.fori_loop(0, tiles, body, 0)
        proj = lax.dot_general(
            gath[origin], pw_ref[:, pl.ds(pl.multiple_of(origin * bw, bw), bw)], (((1,), (1,)), ((), ())),
            preferred_element_type=jnp.float32)
        if fresh:
            pin_ref[...] = proj
        else:
            pin_ref[...] += proj

    def own():
        load = w_load(me, 0)
        load.start()
        load.wait()

        def body(t, top):
            gacc[:, cols_of(t)] = partial_tile(0, slice(None), t)
            return top

        lax.fori_loop(0, tiles, body, 0)
        forward(me, 0, True)

    def ring(r, top):
        from_left, from_right = me - r, me + r
        ag_l, ag_r = (r > 0) & (from_left >= 0), (r > 0) & (from_right < n)
        late_r, late_l = r - me, r - (n - 1 - me)
        d_r, d_l = n - 1 - late_r, late_l
        send_r = (late_r >= 0) & (d_r > me)
        send_l = (late_l >= 0) & (d_l < me)

        @pl.when(send_r)
        def _():
            w_load(d_r, 0).start()

        @pl.when(send_l)
        def _():
            w_load(d_l, 1).start()

        def pass_on(c, top):
            @pl.when(ag_l)
            def _():
                ag_wait(from_left, c)

                @pl.when(has_right)
                def _():
                    ag_copy(from_left + 1, c, 1).wait_send()
                    ag_copy(from_left, c, 1).start()

            @pl.when(ag_r)
            def _():
                ag_wait(from_right, c)

                @pl.when(has_left)
                def _():
                    ag_copy(from_right - 1, c, -1).wait_send()
                    ag_copy(from_right, c, -1).start()

            return top

        lax.fori_loop(0, CHUNKS, pass_on, 0)

        @pl.when(send_r)
        def _():
            w_load(d_r, 0).wait()

        @pl.when(send_l)
        def _():
            w_load(d_l, 1).wait()

        def chunk(c, top):
            @pl.when(send_r)
            def _():
                rs_task(d_r, c, 1, 0, has_left, late_r == 0)

            @pl.when(send_l)
            def _():
                rs_task(d_l, c, -1, 1, has_right, late_l == 0)

            return top

        lax.fori_loop(0, CHUNKS, chunk, 0)

        @pl.when(ag_l)
        def _():
            w_load(from_left, 0).start()

        @pl.when(ag_r)
        def _():
            w_load(from_right, 1).start()

        @pl.when(ag_l)
        def _():
            w_load(from_left, 0).wait()
            forward(from_left, 0)

        @pl.when(ag_r)
        def _():
            w_load(from_right, 1).wait()
            forward(from_right, 1)
        return top

    own()
    lax.fori_loop(0, n, ring, 0)

    def result(t, top):
        lay_ref[:, cols_of(t)] = acc[:, cols_of(t)].astype(lay_ref.dtype)
        return top

    lax.fori_loop(0, tiles, result, 0)

    def finish(c, top):
        rows = rows_of(c)

        @pl.when(has_left)
        def _():
            rs_last(c, me)

        @pl.when(has_right)
        def _():
            rs_last(c, n)

        def narrowed(t, top):
            grad_ref[rows, cols_of(t)] = gacc[rows, cols_of(t)].astype(grad_ref.dtype)
            return top

        lax.fori_loop(0, tiles, narrowed, 0)
        return top

    lax.fori_loop(0, CHUNKS, finish, 0)

    for c in range(CHUNKS):
        @pl.when(has_right)
        def _():
            for copy in rs_copies(me + 1, c, 1):
                copy.wait_send()

        @pl.when(has_left)
        def _():
            for copy in rs_copies(me - 1, c, -1):
                copy.wait_send()


def both_products(n, attn_out, cotangent, out_weight, proj_in_t):
    tok, bw = attn_out.shape
    narrow = n <= 8
    wire = jnp.int16 if narrow else jnp.float32
    cr = tok // CHUNKS
    dma = pltpu.SemaphoreType.DMA
    out = jax.ShapeDtypeStruct((tok, bw), jnp.bfloat16)
    return pl.pallas_call(
        functools.partial(kernel, n, narrow),
        out_shape=(out, out, jax.ShapeDtypeStruct((tok, proj_in_t.shape[0]), jnp.float32)),
        in_specs=[pl.BlockSpec(memory_space=pl.ANY)] * 3 + [pl.BlockSpec(memory_space=pltpu.VMEM)],
        out_specs=(pl.BlockSpec(memory_space=pltpu.VMEM),) * 3,
        scratch_shapes=[
            pltpu.VMEM((n, tok, bw), jnp.bfloat16),
            pltpu.VMEM((tok, bw), jnp.bfloat16),
            pltpu.VMEM((2, bw, bw), jnp.bfloat16),
            pltpu.VMEM((tok, bw), jnp.float32),
            pltpu.VMEM((tok, bw), jnp.float32),
            pltpu.VMEM((cr, bw), jnp.float32),
            pltpu.VMEM((n + 1, tok, bw), wire),
            pltpu.VMEM((n - 1, tok, bw), wire),
            pltpu.VMEM((n + 1, CHUNKS, 8, cr), jnp.float32),
            pltpu.VMEM((n - 1, CHUNKS, 8, cr), jnp.float32),
            dma((2,)),
            dma((2,)),
            dma((n, CHUNKS)),
            dma((n, CHUNKS)),
            dma((n, CHUNKS)),
            dma((n + 1, CHUNKS)),
            dma((n - 1, CHUNKS)),
            dma((n + 1, CHUNKS)),
            dma((n - 1, CHUNKS)),
        ],
        compiler_params=pltpu.CompilerParams(
            collective_id=0, has_side_effects=True, vmem_limit_bytes=62 * 1024 * 1024
        ),
        cost_estimate=pl.CostEstimate(
            flops=4 * n * tok * bw * bw, bytes_accessed=400 * 1024 * 1024, transcendentals=0
        ),
    )(attn_out, cotangent, out_weight, proj_in_t)


def per_device(n, attn_out, out_weight, cotangent, proj_in_w, proj_out_w, queries, lengths):
    tok_rows = attn_out.shape[0]
    block_width = attn_out.shape[1]
    rank_width = proj_in_w.shape[1]
    seq_count = lengths.shape[0]
    block_start = lax.axis_index("mp") * block_width
    local_out_w = lax.dynamic_slice_in_dim(proj_out_w, block_start, block_width, 0)
    part_out = jnp.dot(cotangent, local_out_w, preferred_element_type=jnp.float32)
    proj_out = lax.psum(part_out, "mp")
    layer_out, grad_in, proj_in = both_products(n, attn_out, cotangent, out_weight, proj_in_w.T)
    slot_index = jnp.arange(tok_rows, dtype=jnp.int32)
    example_ids = slot_index // LEN
    offsets = slot_index % LEN
    seq_slots = jnp.arange(seq_count, dtype=jnp.int32)
    live_table = (example_ids[:, None] == seq_slots[None, :]) & (
        offsets[:, None] < lengths[None, :]
    )
    live_rows = jnp.sum(live_table.astype(jnp.float32), axis=1)
    weighted = (proj_in * live_rows[:, None]).reshape(seq_count, LEN, rank_width)
    kronecker = jnp.einsum(
        "eti,etj->eij",
        weighted,
        proj_out.reshape(seq_count, LEN, rank_width),
        precision=HIGHEST_PRECISION,
    ).reshape(seq_count, rank_width * rank_width)
    high = lax.reduce_precision(kronecker, 8, 7)
    middle = lax.reduce_precision(kronecker - high, 8, 7)
    low = kronecker - high - middle
    terms = jnp.concatenate([high, middle, low], axis=0).astype(jnp.bfloat16)
    products = lax.dot_general(
        terms,
        lax.all_gather(queries, "dp", axis=1, tiled=True),
        (((1,), (1,)), ((), ())),
        preferred_element_type=jnp.float32,
    )
    scores = jnp.sum(products.reshape(3, seq_count, -1), axis=0)
    return (layer_out, grad_in, scores)


def solution(mesh):
    in_specs = (
        P(("groups", "dp"), "mp"),
        P(None, "mp"),
        P(("groups", "dp"), "mp"),
        P(),
        P(),
        P("mp", "dp"),
        P(("groups", "dp")),
    )
    out_specs = (P(("groups", "dp"), "mp"), P(("groups", "dp"), "mp"), P(("groups", "dp"), "mp"))
    return jax.shard_map(
        functools.partial(per_device, mesh.shape["mp"]),
        mesh=mesh, in_specs=in_specs, out_specs=out_specs, check_vma=False,
    )
```

```python
import functools

import jax
import jax.numpy as jnp
from jax import lax
from jax.experimental import pallas as pl
from jax.experimental.pallas import tpu as pltpu
from jax.sharding import PartitionSpec as P

LEN = 256
CHUNKS = 4
STEPS = 32767.0
MESH = pl.DeviceIdType.MESH

HIGHEST_PRECISION = lax.Precision.HIGHEST


def kernel(n, narrow, attn_hbm, cot_hbm, w_hbm, pw_ref, lay_ref, grad_ref, pin_ref, gath, cot, wbuf, acc, gacc, tmp, rs, stage,
           sc, sstage, in_sem, w_sem, ag_recv, ag_send_r, ag_send_l, rs_recv, rs_send, sc_recv, sc_send):
    me = lax.axis_index("mp")
    tok, bw = cot.shape
    cr = tok // CHUNKS
    tn = min(256, bw)
    tiles = bw // tn

    def rows_of(c):
        return pl.ds(pl.multiple_of(c * cr, cr), cr)

    def cols_of(t):
        return pl.ds(pl.multiple_of(t * tn, tn), tn)

    def w_load(block, slot):
        return pltpu.make_async_copy(
            w_hbm.at[pl.ds(pl.multiple_of(block * bw, bw), bw), :], wbuf.at[slot], w_sem.at[slot])

    attn_in = pltpu.make_async_copy(attn_hbm, gath.at[me], in_sem.at[0])
    cot_in = pltpu.make_async_copy(cot_hbm, cot, in_sem.at[1])
    attn_in.start()
    cot_in.start()

    barrier = pltpu.get_barrier_semaphore()
    has_left, has_right = me > 0, me < n - 1

    @pl.when(has_left)
    def _():
        pl.semaphore_signal(barrier, inc=1, device_id={"mp": me - 1}, device_id_type=MESH)

    @pl.when(has_right)
    def _():
        pl.semaphore_signal(barrier, inc=1, device_id={"mp": me + 1}, device_id_type=MESH)

    pl.semaphore_wait(barrier, has_left.astype(jnp.int32) + has_right.astype(jnp.int32))

    def ag_copy(origin, c, side):
        part = gath.at[origin, rows_of(c)]
        sems = ag_send_r if side > 0 else ag_send_l
        return pltpu.make_async_remote_copy(
            src_ref=part, dst_ref=part, send_sem=sems.at[origin, c], recv_sem=ag_recv.at[origin, c],
            device_id={"mp": me + side}, device_id_type=MESH)

    def ag_wait(origin, c):
        part = gath.at[origin, rows_of(c)]
        pltpu.make_async_copy(part, part, ag_recv.at[origin, c]).wait()

    def rs_copies(d, c, side):
        out = d - 1 if side > 0 else d
        there = d if side > 0 else jnp.where(d == me - 1, n, d)
        data = pltpu.make_async_remote_copy(
            src_ref=stage.at[out, rows_of(c)], dst_ref=rs.at[there, rows_of(c)],
            send_sem=rs_send.at[out, c], recv_sem=rs_recv.at[there, c],
            device_id={"mp": me + side}, device_id_type=MESH)
        if not narrow:
            return (data,)
        return (data, pltpu.make_async_remote_copy(
            src_ref=sstage.at[out, c], dst_ref=sc.at[there, c],
            send_sem=sc_send.at[out, c], recv_sem=sc_recv.at[there, c],
            device_id={"mp": me + side}, device_id_type=MESH))

    def rs_wait(slot, c):
        pltpu.make_async_copy(rs.at[slot, rows_of(c)], rs.at[slot, rows_of(c)], rs_recv.at[slot, c]).wait()
        if narrow:
            pltpu.make_async_copy(sc.at[slot, c], sc.at[slot, c], sc_recv.at[slot, c]).wait()

    def scale_of(slot, c):
        wide = jnp.broadcast_to(sc[slot, c][0:1, :], (128, cr))
        return jnp.transpose(wide)[:, 0:1] * (1.0 / STEPS)

    attn_in.wait()
    for c in range(CHUNKS):
        @pl.when(has_right)
        def _():
            ag_copy(me, c, 1).start()

        @pl.when(has_left)
        def _():
            ag_copy(me, c, -1).start()
    cot_in.wait()

    def partial_tile(slot, rows, t):
        return lax.dot_general(
            cot[rows, :], wbuf[slot, cols_of(t), :], (((1,), (1,)), ((), ())),
            preferred_element_type=jnp.float32)

    def rs_task(d, c, side, slot, incoming, opening):
        rows = rows_of(c)
        src = d

        def first(t, top):
            tmp[:, cols_of(t)] = partial_tile(slot, rows, t)
            return top

        lax.fori_loop(0, tiles, first, 0)

        @pl.when(incoming)
        def _():
            rs_wait(src, c)
            scale = scale_of(src, c) if narrow else 1.0

            def add(t, top):
                tmp[:, cols_of(t)] += rs[src, rows, cols_of(t)].astype(jnp.float32) * scale
                return top

            lax.fori_loop(0, tiles, add, 0)

        out = d - 1 if side > 0 else d
        if narrow:
            def most(t, top):
                part = jnp.abs(tmp[:, cols_of(t)])
                for k in range(tn // 128):
                    top = jnp.maximum(top, part[:, k * 128:(k + 1) * 128])
                return top

            top = lax.fori_loop(0, tiles, most, jnp.full((cr, 128), 1e-30, jnp.float32))
            sstage[out, c] = jnp.broadcast_to(jnp.max(jnp.transpose(top), axis=0, keepdims=True), (8, cr))
            inv = STEPS / jnp.max(top, axis=1, keepdims=True)

            def code(t, top):
                stage[out, rows, cols_of(t)] = jnp.round(tmp[:, cols_of(t)] * inv).astype(jnp.int32).astype(jnp.int16)
                return top
        else:
            def code(t, top):
                stage[out, rows, cols_of(t)] = tmp[:, cols_of(t)]
                return top

        lax.fori_loop(0, tiles, code, 0)

        @pl.when(opening)
        def _():
            ag_copy(0 if side > 0 else n - 1, c, side).wait_send()

        @pl.when(jnp.logical_not(opening))
        def _():
            for copy in rs_copies(d + side, c, side):
                copy.wait_send()

        for copy in rs_copies(d, c, side):
            copy.start()

    def rs_last(c, slot):
        rows = rows_of(c)
        rs_wait(slot, c)
        scale = scale_of(slot, c) if narrow else 1.0

        def add(t, top):
            gacc[rows, cols_of(t)] += rs[slot, rows, cols_of(t)].astype(jnp.float32) * scale
            return top

        lax.fori_loop(0, tiles, add, 0)

    def forward(origin, slot, fresh=False):
        def body(t, top):
            part = jnp.dot(gath[origin], wbuf[slot, :, cols_of(t)], preferred_element_type=jnp.float32)
            if fresh:
                acc[:, cols_of(t)] = part
            else:
                acc[:, cols_of(t)] += part
            return top

        lax.fori_loop(0, tiles, body, 0)
        proj = lax.dot_general(
            gath[origin], pw_ref[:, pl.ds(pl.multiple_of(origin * bw, bw), bw)], (((1,), (1,)), ((), ())),
            preferred_element_type=jnp.float32)
        if fresh:
            pin_ref[...] = proj
        else:
            pin_ref[...] += proj

    def own():
        load = w_load(me, 0)
        load.start()
        load.wait()

        def body(t, top):
            gacc[:, cols_of(t)] = partial_tile(0, slice(None), t)
            return top

        lax.fori_loop(0, tiles, body, 0)
        forward(me, 0, True)

    def ring(r, top):
        from_left, from_right = me - r, me + r
        ag_l, ag_r = (r > 0) & (from_left >= 0), (r > 0) & (from_right < n)
        late_r, late_l = r - me, r - (n - 1 - me)
        d_r, d_l = n - 1 - late_r, late_l
        send_r = (late_r >= 0) & (d_r > me)
        send_l = (late_l >= 0) & (d_l < me)

        @pl.when(ag_l)
        def _():
            w_load(from_left, 0).start()

        @pl.when(ag_r)
        def _():
            w_load(from_right, 1).start()

        def pass_on(c, top):
            @pl.when(ag_l)
            def _():
                ag_wait(from_left, c)

                @pl.when(has_right)
                def _():
                    ag_copy(from_left + 1, c, 1).wait_send()
                    ag_copy(from_left, c, 1).start()

            @pl.when(ag_r)
            def _():
                ag_wait(from_right, c)

                @pl.when(has_left)
                def _():
                    ag_copy(from_right - 1, c, -1).wait_send()
                    ag_copy(from_right, c, -1).start()

            return top

        lax.fori_loop(0, CHUNKS, pass_on, 0)

        @pl.when(ag_l)
        def _():
            w_load(from_left, 0).wait()
            forward(from_left, 0)

        @pl.when(ag_r)
        def _():
            w_load(from_right, 1).wait()
            forward(from_right, 1)

        @pl.when(send_r)
        def _():
            w_load(d_r, 0).start()

        @pl.when(send_l)
        def _():
            w_load(d_l, 1).start()

        @pl.when(send_r)
        def _():
            w_load(d_r, 0).wait()

        @pl.when(send_l)
        def _():
            w_load(d_l, 1).wait()

        def chunk(c, top):
            @pl.when(send_r)
            def _():
                rs_task(d_r, c, 1, 0, has_left, late_r == 0)

            @pl.when(send_l)
            def _():
                rs_task(d_l, c, -1, 1, has_right, late_l == 0)

            return top

        lax.fori_loop(0, CHUNKS, chunk, 0)
        return top

    own()
    lax.fori_loop(0, n, ring, 0)

    def result(t, top):
        lay_ref[:, cols_of(t)] = acc[:, cols_of(t)].astype(lay_ref.dtype)
        return top

    lax.fori_loop(0, tiles, result, 0)

    def finish(c, top):
        rows = rows_of(c)

        @pl.when(has_left)
        def _():
            rs_last(c, me)

        @pl.when(has_right)
        def _():
            rs_last(c, n)

        def narrowed(t, top):
            grad_ref[rows, cols_of(t)] = gacc[rows, cols_of(t)].astype(grad_ref.dtype)
            return top

        lax.fori_loop(0, tiles, narrowed, 0)
        return top

    lax.fori_loop(0, CHUNKS, finish, 0)

    for c in range(CHUNKS):
        @pl.when(has_right)
        def _():
            for copy in rs_copies(me + 1, c, 1):
                copy.wait_send()

        @pl.when(has_left)
        def _():
            for copy in rs_copies(me - 1, c, -1):
                copy.wait_send()


def both_products(n, attn_out, cotangent, out_weight, proj_in_t):
    tok, bw = attn_out.shape
    narrow = n <= 8
    wire = jnp.int16 if narrow else jnp.float32
    cr = tok // CHUNKS
    dma = pltpu.SemaphoreType.DMA
    out = jax.ShapeDtypeStruct((tok, bw), jnp.bfloat16)
    return pl.pallas_call(
        functools.partial(kernel, n, narrow),
        out_shape=(out, out, jax.ShapeDtypeStruct((tok, proj_in_t.shape[0]), jnp.float32)),
        in_specs=[pl.BlockSpec(memory_space=pl.ANY)] * 3 + [pl.BlockSpec(memory_space=pltpu.VMEM)],
        out_specs=(pl.BlockSpec(memory_space=pltpu.VMEM),) * 3,
        scratch_shapes=[
            pltpu.VMEM((n, tok, bw), jnp.bfloat16),
            pltpu.VMEM((tok, bw), jnp.bfloat16),
            pltpu.VMEM((2, bw, bw), jnp.bfloat16),
            pltpu.VMEM((tok, bw), jnp.float32),
            pltpu.VMEM((tok, bw), jnp.float32),
            pltpu.VMEM((cr, bw), jnp.float32),
            pltpu.VMEM((n + 1, tok, bw), wire),
            pltpu.VMEM((n - 1, tok, bw), wire),
            pltpu.VMEM((n + 1, CHUNKS, 8, cr), jnp.float32),
            pltpu.VMEM((n - 1, CHUNKS, 8, cr), jnp.float32),
            dma((2,)),
            dma((2,)),
            dma((n, CHUNKS)),
            dma((n, CHUNKS)),
            dma((n, CHUNKS)),
            dma((n + 1, CHUNKS)),
            dma((n - 1, CHUNKS)),
            dma((n + 1, CHUNKS)),
            dma((n - 1, CHUNKS)),
        ],
        compiler_params=pltpu.CompilerParams(
            collective_id=0, has_side_effects=True, vmem_limit_bytes=62 * 1024 * 1024
        ),
        cost_estimate=pl.CostEstimate(
            flops=4 * n * tok * bw * bw, bytes_accessed=400 * 1024 * 1024, transcendentals=0
        ),
    )(attn_out, cotangent, out_weight, proj_in_t)


def per_device(n, attn_out, out_weight, cotangent, proj_in_w, proj_out_w, queries, lengths):
    tok_rows = attn_out.shape[0]
    block_width = attn_out.shape[1]
    rank_width = proj_in_w.shape[1]
    seq_count = lengths.shape[0]
    block_start = lax.axis_index("mp") * block_width
    local_out_w = lax.dynamic_slice_in_dim(proj_out_w, block_start, block_width, 0)
    part_out = jnp.dot(cotangent, local_out_w, preferred_element_type=jnp.float32)
    proj_out = lax.psum(part_out, "mp")
    layer_out, grad_in, proj_in = both_products(n, attn_out, cotangent, out_weight, proj_in_w.T)
    slot_index = jnp.arange(tok_rows, dtype=jnp.int32)
    example_ids = slot_index // LEN
    offsets = slot_index % LEN
    seq_slots = jnp.arange(seq_count, dtype=jnp.int32)
    live_table = (example_ids[:, None] == seq_slots[None, :]) & (
        offsets[:, None] < lengths[None, :]
    )
    live_rows = jnp.sum(live_table.astype(jnp.float32), axis=1)
    weighted = (proj_in * live_rows[:, None]).reshape(seq_count, LEN, rank_width)
    kronecker = jnp.einsum(
        "eti,etj->eij",
        weighted,
        proj_out.reshape(seq_count, LEN, rank_width),
        precision=HIGHEST_PRECISION,
    ).reshape(seq_count, rank_width * rank_width)
    high = lax.reduce_precision(kronecker, 8, 7)
    middle = lax.reduce_precision(kronecker - high, 8, 7)
    low = kronecker - high - middle
    terms = jnp.concatenate([high, middle, low], axis=0).astype(jnp.bfloat16)
    products = lax.dot_general(
        terms,
        lax.all_gather(queries, "dp", axis=1, tiled=True),
        (((1,), (1,)), ((), ())),
        preferred_element_type=jnp.float32,
    )
    scores = jnp.sum(products.reshape(3, seq_count, -1), axis=0)
    return (layer_out, grad_in, scores)


def solution(mesh):
    in_specs = (
        P(("groups", "dp"), "mp"),
        P(None, "mp"),
        P(("groups", "dp"), "mp"),
        P(),
        P(),
        P("mp", "dp"),
        P(("groups", "dp")),
    )
    out_specs = (P(("groups", "dp"), "mp"), P(("groups", "dp"), "mp"), P(("groups", "dp"), "mp"))
    return jax.shard_map(
        functools.partial(per_device, mesh.shape["mp"]),
        mesh=mesh, in_specs=in_specs, out_specs=out_specs, check_vma=False,
    )
```
